32 devices in a mesh: blk: 8 (over z, x), panel: 4 (over y, core).
Axes of the slice: x: 2, y: 2, z: 4, core: 2. Of those that a mesh axis runs over, the one named last changes fastest.
Arguments:
- points: float32 [128, 6144], P(None, 'blk'), may hold values from -40 to 40
- lengthscale: float32 [128], replicated, may hold values from 5.656854 to 22.627417
- noise_level: float32 [1], replicated, may hold values from 0.5 to 1.5
- right_sides: float32 [17, 6144], P(None, 'blk'), may hold values from -6 to 6
- pivots: int32 [256], P('panel'), may hold values from 0 to 6143, as said below
Outputs:
- solution: float32 [17, 6144], P(None, 'blk')
- residual: float32 [17, 6144], P(None, 'blk')
The draws below stay inside these ranges and needn't reach their ends.
Inputs may be any that keep to these rules, and one draw needn't show every extreme that they name: `pivots`: 256 distinct point indices; 0 and 6143 are always among them.
All inputs are finite; a program needn't handle non-finite values.
Results may differ from the reference program's by a relative error of at most 0.0003.
Values sent between devices are 32-bit elements; how exact they have to be, the bound alone decides.
A program may use at most 128 MiB of HBM per device.

```python
import math
import jax
import jax.numpy as jnp
from jax import lax

F = 128
RANK = 256
ITERS = 2
ROWS = 768
VEC = 17
N = 6144
N_BLK = 8


def draw_points(key, part):
    key = jax.random.fold_in(key, 7)
    mix_key, latent_key, jitter_key = jax.random.split(key, 3)
    latent_count = 8
    mixing = jax.random.uniform(mix_key, (F, latent_count), jnp.float32, -1.7, 1.7)
    latent = jax.random.uniform(latent_key, (latent_count, N), jnp.float32, -1.7, 1.7)
    jitter = jnp.clip(jax.random.normal(jitter_key, (F, N), jnp.float32), -4.0, 4.0)
    summed = jitter
    for column in range(latent_count):
        summed = summed + mixing[:, column:column + 1] * latent[column:column + 1, :]
    return summed.astype(jnp.float32)


def draw_pivots(key, part):
    key = jax.random.fold_in(key, 5)
    first_key, second_key = jax.random.split(key)
    middle = jax.random.permutation(first_key, N - 2)[:RANK - 2].astype(jnp.int32) + 1
    chosen = jnp.concatenate([jnp.array([0, N - 1], jnp.int32), middle])
    order = jax.random.permutation(second_key, RANK)
    return chosen[order].astype(jnp.int32)


def block_levels(stream_key, extent, cuts, smallest, top_value):
    loudness = 1.0
    for position, shards_of in cuts:
        heights = jax.random.uniform(jax.random.fold_in(jax.random.fold_in(stream_key, 6), position), (shards_of,), jnp.float32, smallest / len(cuts), top_value / len(cuts))
        loudness = loudness * jnp.repeat(jnp.exp(heights), extent[position] // shards_of).reshape((-1,) + (1,) * (len(extent) - 1 - position))
    return loudness


def scatter_about(stream_key, extent, width, limit, cuts=(), held_as=jnp.bfloat16):
    drawn = jax.random.normal(stream_key, extent, jnp.float32) * width
    if len(cuts) > 0:
        drawn = block_levels(stream_key, extent, cuts, -0.22, 0.18) * drawn
    return jnp.clip(drawn, min=-limit, max=limit).astype(held_as)


def setup_inputs(seed: int = 0) -> dict:
    streams_of = jax.random.split(jax.random.key(seed), 6)
    return {
        "points": draw_points(jax.random.fold_in(streams_of[5], 71), 0),
        "lengthscale": jnp.clip(jnp.exp(jax.random.uniform(streams_of[1], (F,), jnp.float32, math.log(5.656854), math.log(22.627417))), 5.656854, 22.627417),
        "noise_level": jnp.clip(jax.random.uniform(streams_of[2], (1,), jnp.float32, 0.5, 1.5), 0.5, 1.5),
        "right_sides": scatter_about(streams_of[3], (VEC, N), 1.0, 6.0, ((1, 8),), jnp.float32),
        "pivots": draw_pivots(jax.random.fold_in(streams_of[5], 71), 0),
    }


HIGH = lax.Precision.HIGHEST

def kernel_block(left_pts, right_pts):
    cross_terms = lax.dot_general(left_pts.astype(jnp.float32), right_pts.astype(jnp.float32), (((0,), (0,)), ((), ())), precision=HIGH, preferred_element_type=jnp.float32)
    left_sq = jnp.sum(left_pts * left_pts, axis=0)
    right_sq = jnp.sum(right_pts * right_pts, axis=0)
    return jnp.exp(-0.5 * (left_sq[:, None] + right_sq[None, :] - 2.0 * cross_terms))

def reference(points, lengthscale, noise_level, right_sides, pivots):
    scaled = points / lengthscale[:, None]
    noise = noise_level[0]
    pivot_cols = scaled[:, pivots]
    panel_rows = kernel_block(pivot_cols, scaled)
    inner_kernel = kernel_block(pivot_cols, pivot_cols)
    gram = jnp.dot(panel_rows.astype(jnp.float32), panel_rows.T.astype(jnp.float32), precision=HIGH, preferred_element_type=jnp.float32)
    factor = jnp.linalg.cholesky(noise * inner_kernel + gram)
    blocks = scaled.reshape(scaled.shape[0], N_BLK, ROWS).transpose(1, 0, 2)

    def operator(direction):

        def one_block(block_pts):
            kernel_tile = kernel_block(scaled, block_pts)
            return jnp.dot(direction.astype(jnp.float32), kernel_tile.astype(jnp.float32), precision=HIGH, preferred_element_type=jnp.float32)
        pieces = lax.map(one_block, blocks)
        return pieces.transpose(1, 0, 2).reshape(direction.shape) + noise * direction

    def precondition(resid):
        projected = jnp.dot(panel_rows.astype(jnp.float32), resid.T.astype(jnp.float32), precision=HIGH, preferred_element_type=jnp.float32)
        coefficients = jax.scipy.linalg.cho_solve((factor, True), projected)
        return (resid - jnp.dot(coefficients.T.astype(jnp.float32), panel_rows.astype(jnp.float32), precision=HIGH, preferred_element_type=jnp.float32)) / noise
    solution = jnp.zeros_like(right_sides)
    residual = right_sides
    direction = precondition(residual)
    precond_norm = jnp.sum(residual * direction, axis=1)
    for iteration in range(ITERS):
        images = operator(direction)
        step_size = precond_norm / jnp.sum(direction * images, axis=1)
        solution = solution + step_size[:, None] * direction
        residual = residual - step_size[:, None] * images
        if iteration + 1 < ITERS:
            preconditioned = precondition(residual)
            new_norm = jnp.sum(residual * preconditioned, axis=1)
            direction = preconditioned + (new_norm / precond_norm)[:, None] * direction
            precond_norm = new_norm
    return (solution, residual)
```

```python
import functools

import jax
import jax.numpy as jnp
from jax import lax
from jax.experimental import pallas as pl
from jax.experimental.pallas import tpu as pltpu
from jax.sharding import PartitionSpec as P

HIGH = lax.Precision.HIGHEST
VMEM = pl.BlockSpec(memory_space=pltpu.VMEM)
MESH = pl.DeviceIdType.MESH
VMEM_BYTES = 48 * 1024 * 1024


def dot(left, right, left_dim, right_dim):
    return lax.dot_general(
        left,
        right,
        (((left_dim,), (right_dim,)), ((), ())),
        precision=HIGH,
        preferred_element_type=jnp.float32,
    )


def gather_kernel(axis, size, count, *refs):
    ins, outs = refs[:count], refs[count : 2 * count]
    send_sem, recv_sem = refs[2 * count :]
    me = lax.axis_index(axis)
    barrier = pltpu.get_barrier_semaphore()
    for hop in range(1, size):
        pl.semaphore_signal(
            barrier, inc=1, device_id={axis: lax.rem(me + hop, size)}, device_id_type=MESH
        )
    pl.semaphore_wait(barrier, size - 1)

    def copy_of(item, hop, slot):
        return pltpu.make_async_remote_copy(
            src_ref=ins[item],
            dst_ref=outs[item].at[slot],
            send_sem=send_sem.at[item, hop],
            recv_sem=recv_sem.at[item, hop],
            device_id={axis: lax.rem(me + hop, size)},
            device_id_type=MESH,
        )

    for hop in range(size - 1, 0, -1):
        for item in range(count):
            copy_of(item, hop, me).start()
    for item in range(count):
        outs[item][me] = ins[item][...]
    for hop in range(1, size):
        for item in range(count):
            copy_of(item, hop, lax.rem(me + size - hop, size)).wait_recv()
    for hop in range(1, size):
        for item in range(count):
            copy_of(item, hop, me).wait_send()


def gather(arrays, axis, collective_id):
    size = lax.axis_size(axis)
    count = len(arrays)
    return pl.pallas_call(
        functools.partial(gather_kernel, axis, size, count),
        out_shape=[jax.ShapeDtypeStruct((size,) + a.shape, a.dtype) for a in arrays],
        in_specs=[VMEM] * count,
        out_specs=[VMEM] * count,
        scratch_shapes=[
            pltpu.SemaphoreType.DMA((count, size)),
            pltpu.SemaphoreType.DMA((count, size)),
        ],
        compiler_params=pltpu.CompilerParams(
            collective_id=collective_id, has_side_effects=True, vmem_limit_bytes=VMEM_BYTES
        ),
    )(*arrays)


def sum_kernel(axis, steps, count, *refs):
    ins, outs = refs[:count], refs[count : 2 * count]
    landed = refs[2 * count : 3 * count]
    send_sem, recv_sem = refs[3 * count :]
    me = lax.axis_index(axis)
    partners = [me + s * (1 - 2 * lax.rem(me // s, 2)) for s in steps]
    barrier = pltpu.get_barrier_semaphore()
    for partner in partners:
        pl.semaphore_signal(barrier, inc=1, device_id={axis: partner}, device_id_type=MESH)
    pl.semaphore_wait(barrier, len(steps))
    held = list(ins)
    for step, partner in enumerate(partners):
        copies = []
        for item in range(count):
            copy = pltpu.make_async_remote_copy(
                src_ref=held[item],
                dst_ref=landed[item].at[step],
                send_sem=send_sem.at[item, step],
                recv_sem=recv_sem.at[item, step],
                device_id={axis: partner},
                device_id_type=MESH,
            )
            copy.start()
            copies.append(copy)
        for item in range(count):
            copies[item].wait()
            outs[item][...] = held[item][...] + landed[item][step]
            held[item] = outs[item]


def sum_over(arrays, axis, collective_id):
    size = lax.axis_size(axis)
    steps = []
    while (1 << len(steps)) < size:
        steps.append(1 << len(steps))
    count = len(arrays)
    return pl.pallas_call(
        functools.partial(sum_kernel, axis, steps, count),
        out_shape=[jax.ShapeDtypeStruct(a.shape, a.dtype) for a in arrays],
        in_specs=[VMEM] * count,
        out_specs=[VMEM] * count,
        scratch_shapes=[pltpu.VMEM((len(steps),) + a.shape, a.dtype) for a in arrays]
        + [
            pltpu.SemaphoreType.DMA((count, len(steps))),
            pltpu.SemaphoreType.DMA((count, len(steps))),
        ],
        compiler_params=pltpu.CompilerParams(
            collective_id=collective_id, has_side_effects=True, vmem_limit_bytes=VMEM_BYTES
        ),
    )(*arrays)


def kern(left, left_sq, right, right_dim, right_sq):
    cross = dot(left, right, 1, right_dim)
    return jnp.exp(-0.5 * (left_sq[:, None] + right_sq[None, :] - 2.0 * cross))


def per_device(points, lengthscale, noise_level, right_sides, pivots):
    row_count = points.shape[1]
    vec = right_sides.shape[0]
    panel_size = lax.axis_size("panel")
    quarter = row_count // panel_size
    panel_start = lax.axis_index("panel") * quarter
    noise = noise_level[0]
    scaled = points / lengthscale[:, None]
    local_sq = jnp.sum(scaled * scaled, axis=0)
    row_ids = lax.axis_index("blk") * row_count + lax.iota(jnp.int32, row_count)
    onehot = (pivots[:, None] == row_ids[None, :]).astype(jnp.float32)
    picked = dot(onehot, scaled, 1, 1)

    def own_quarter(vectors):
        return lax.dynamic_slice_in_dim(vectors, panel_start, quarter, 1)

    def spread(stacked):
        return stacked.transpose(1, 0, 2).reshape(vec, -1)

    quarter_points, picks, rhs_parts = gather(
        [own_quarter(scaled).T, picked, own_quarter(right_sides)], "blk", 0
    )
    visit = quarter_points.reshape(-1, points.shape[0])
    visit_sq = jnp.sum(visit * visit, axis=1)
    rhs_q = spread(rhs_parts)
    (pivot_parts,) = gather([jnp.sum(picks, axis=0)], "panel", 1)
    pivot_rows = pivot_parts.reshape(-1, points.shape[0])
    pivot_sq = jnp.sum(pivot_rows * pivot_rows, axis=1)

    panel_q = kern(pivot_rows, pivot_sq, visit, 1, visit_sq)
    panel_own = kern(pivot_rows, pivot_sq, scaled, 0, local_sq)
    inner_kernel = kern(pivot_rows, pivot_sq, pivot_rows, 1, pivot_sq)
    tile = kern(visit, visit_sq, scaled, 0, local_sq)

    gram, proj = sum_over([dot(panel_q, panel_q, 1, 1), dot(rhs_q, panel_q, 1, 1)], "panel", 2)
    factor = jnp.linalg.cholesky(noise * inner_kernel + gram)

    def coefficients_of(projected):
        return jax.scipy.linalg.cho_solve((factor, True), projected.T).T

    def precondition(resid, coefficients, panel_rows):
        return (resid - dot(coefficients, panel_rows, 1, 0)) / noise

    coef = coefficients_of(proj)
    dir_q = precondition(rhs_q, coef, panel_q)
    dir_own = precondition(right_sides, coef, panel_own)
    (image_own,) = sum_over([dot(dir_q, tile, 1, 0)], "panel", 3)
    image_own = image_own + noise * dir_own
    (image_parts,) = gather([own_quarter(image_own)], "blk", 4)
    image_q = spread(image_parts)
    lanes = lax.broadcasted_iota(jnp.int32, (1, 128), 1)

    def pack(columns):
        packed = jnp.zeros((vec, 128), jnp.float32)
        for index, column in enumerate(columns):
            packed = jnp.where(lanes == index, column[:, None], packed)
        return packed

    image_proj, dots = sum_over(
        [
            dot(image_q, panel_q, 1, 1),
            pack([jnp.sum(rhs_q * dir_q, axis=1), jnp.sum(dir_q * image_q, axis=1)]),
        ],
        "panel",
        5,
    )
    norm, curvature = dots[:, 0], dots[:, 1]
    step = (norm / curvature)[:, None]
    coef = coefficients_of(proj - step * image_proj)
    resid_own = right_sides - step * image_own
    pre_q = precondition(rhs_q - step * image_q, coef, panel_q)
    pre_own = precondition(resid_own, coef, panel_own)
    (pre_image,) = sum_over([dot(pre_q, tile, 1, 0)], "panel", 6)
    pre_image = pre_image + noise * pre_own
    (dot_parts,) = gather(
        [
            pack(
                [
                    jnp.sum(resid_own * pre_own, axis=1),
                    jnp.sum(pre_own * pre_image, axis=1),
                    jnp.sum(pre_own * image_own + dir_own * pre_image, axis=1),
                ]
            )
        ],
        "blk",
        7,
    )
    dots = jnp.sum(dot_parts, axis=0)
    new_norm = dots[:, 0]
    ratio = new_norm / norm
    curvature = dots[:, 1] + ratio * (dots[:, 2] + ratio * curvature)
    last = (new_norm / curvature)[:, None]
    ratio = ratio[:, None]
    solution = step * dir_own + last * (pre_own + ratio * dir_own)
    residual = resid_own - last * (pre_image + ratio * image_own)
    return (solution, residual)


def solution(mesh):
    return jax.shard_map(
        per_device,
        mesh=mesh,
        in_specs=(P(None, "blk"), P(), P(), P(None, "blk"), P("panel")),
        out_specs=(P(None, "blk"), P(None, "blk")),
        check_vma=False,
    )
```

```python
import functools

import jax
import jax.numpy as jnp
from jax import lax
from jax.experimental import pallas as pl
from jax.experimental.pallas import tpu as pltpu
from jax.sharding import PartitionSpec as P

HIGH = lax.Precision.HIGHEST
VMEM = pl.BlockSpec(memory_space=pltpu.VMEM)
MESH = pl.DeviceIdType.MESH
VMEM_BYTES = 48 * 1024 * 1024


def dot(left, right, left_dim, right_dim):
    return lax.dot_general(
        left,
        right,
        (((left_dim,), (right_dim,)), ((), ())),
        precision=HIGH,
        preferred_element_type=jnp.float32,
    )


def gather_kernel(axis, size, count, *refs):
    ins, outs = refs[:count], refs[count : 2 * count]
    send_sem, recv_sem = refs[2 * count :]
    me = lax.axis_index(axis)
    barrier = pltpu.get_barrier_semaphore()
    for hop in range(1, size):
        pl.semaphore_signal(
            barrier, inc=1, device_id={axis: lax.rem(me + hop, size)}, device_id_type=MESH
        )
    pl.semaphore_wait(barrier, size - 1)

    def copy_of(item, hop, slot):
        return pltpu.make_async_remote_copy(
            src_ref=ins[item],
            dst_ref=outs[item].at[slot],
            send_sem=send_sem.at[item, hop],
            recv_sem=recv_sem.at[item, hop],
            device_id={axis: lax.rem(me + hop, size)},
            device_id_type=MESH,
        )

    for hop in range(size - 1, 0, -1):
        for item in range(count):
            copy_of(item, hop, me).start()
    for item in range(count):
        outs[item][me] = ins[item][...]
    for hop in range(1, size):
        for item in range(count):
            copy_of(item, hop, lax.rem(me + size - hop, size)).wait_recv()
    for hop in range(1, size):
        for item in range(count):
            copy_of(item, hop, me).wait_send()


def gather(arrays, axis, collective_id):
    size = lax.axis_size(axis)
    count = len(arrays)
    return pl.pallas_call(
        functools.partial(gather_kernel, axis, size, count),
        out_shape=[jax.ShapeDtypeStruct((size,) + a.shape, a.dtype) for a in arrays],
        in_specs=[VMEM] * count,
        out_specs=[VMEM] * count,
        scratch_shapes=[
            pltpu.SemaphoreType.DMA((count, size)),
            pltpu.SemaphoreType.DMA((count, size)),
        ],
        compiler_params=pltpu.CompilerParams(
            collective_id=collective_id, has_side_effects=True, vmem_limit_bytes=VMEM_BYTES
        ),
    )(*arrays)


def sum_kernel(axis, steps, count, *refs):
    ins, outs = refs[:count], refs[count : 2 * count]
    landed = refs[2 * count : 3 * count]
    send_sem, recv_sem = refs[3 * count :]
    me = lax.axis_index(axis)
    partners = [me + s * (1 - 2 * lax.rem(me // s, 2)) for s in steps]
    barrier = pltpu.get_barrier_semaphore()
    for partner in partners:
        pl.semaphore_signal(barrier, inc=1, device_id={axis: partner}, device_id_type=MESH)
    pl.semaphore_wait(barrier, len(steps))
    held = list(ins)
    for step, partner in enumerate(partners):
        copies = []
        for item in range(count):
            copy = pltpu.make_async_remote_copy(
                src_ref=held[item],
                dst_ref=landed[item].at[step],
                send_sem=send_sem.at[item, step],
                recv_sem=recv_sem.at[item, step],
                device_id={axis: partner},
                device_id_type=MESH,
            )
            copy.start()
            copies.append(copy)
        for item in range(count):
            copies[item].wait()
            outs[item][...] = held[item][...] + landed[item][step]
            held[item] = outs[item]


def sum_over(arrays, axis, collective_id):
    size = lax.axis_size(axis)
    steps = []
    while (1 << len(steps)) < size:
        steps.append(1 << len(steps))
    count = len(arrays)
    return pl.pallas_call(
        functools.partial(sum_kernel, axis, steps, count),
        out_shape=[jax.ShapeDtypeStruct(a.shape, a.dtype) for a in arrays],
        in_specs=[VMEM] * count,
        out_specs=[VMEM] * count,
        scratch_shapes=[pltpu.VMEM((len(steps),) + a.shape, a.dtype) for a in arrays]
        + [
            pltpu.SemaphoreType.DMA((count, len(steps))),
            pltpu.SemaphoreType.DMA((count, len(steps))),
        ],
        compiler_params=pltpu.CompilerParams(
            collective_id=collective_id, has_side_effects=True, vmem_limit_bytes=VMEM_BYTES
        ),
    )(*arrays)


def inverse_kernel(side, part, width, a_ref, out_ref):
    sub = lax.broadcasted_iota(jnp.int32, (part, part), 0)
    lane = lax.broadcasted_iota(jnp.int32, (part, part), 1)
    head = lax.broadcasted_iota(jnp.int32, (1, part), 1)
    out_ref[...] = a_ref[...]

    def block_step(_, carry):
        block = out_ref[:part, :part]
        for first in range(0, part, width):
            columns = [
                jnp.broadcast_to(block[:, k : k + 1], (part, part))
                for k in range(first, first + width)
            ]
            for index in range(width):
                k = first + index
                here = sub == k
                column = columns[index]
                scale = 1.0 / column[k : k + 1, :]
                row = jnp.where(head == k, 1.0, block[k : k + 1, :]) * scale
                factor = jnp.where(here, -1.0, column)
                block = jnp.where(here | (lane == k), 0.0, block) - factor * row
                for later in range(index + 1, width):
                    entry = columns[later][k : k + 1, :] * scale
                    columns[later] = jnp.where(here, 0.0, columns[later]) - factor * entry
        left = out_ref[part:, :part]
        right = dot(block, out_ref[:part, part:], 1, 0)
        rest = out_ref[part:, part:] - dot(left, right, 1, 0)
        side_part = -dot(left, block, 1, 0)
        out_ref[...] = jnp.concatenate(
            [
                jnp.concatenate([rest, side_part], axis=1),
                jnp.concatenate([right, block], axis=1),
            ],
            axis=0,
        )
        return carry

    lax.fori_loop(0, side // part, block_step, 0)


def inverse_of(matrix):
    side = matrix.shape[0]
    return pl.pallas_call(
        functools.partial(inverse_kernel, side, 64, 8),
        out_shape=jax.ShapeDtypeStruct(matrix.shape, matrix.dtype),
        in_specs=[VMEM],
        out_specs=VMEM,
        compiler_params=pltpu.CompilerParams(vmem_limit_bytes=VMEM_BYTES),
    )(matrix)


def kern(left, left_sq, right, right_dim, right_sq):
    cross = dot(left, right, 1, right_dim)
    return jnp.exp(-0.5 * (left_sq[:, None] + right_sq[None, :] - 2.0 * cross))


def per_device(points, lengthscale, noise_level, right_sides, pivots):
    row_count = points.shape[1]
    vec = right_sides.shape[0]
    panel_size = lax.axis_size("panel")
    quarter = row_count // panel_size
    panel_start = lax.axis_index("panel") * quarter
    noise = noise_level[0]
    scaled = points / lengthscale[:, None]
    local_sq = jnp.sum(scaled * scaled, axis=0)
    row_ids = lax.axis_index("blk") * row_count + lax.iota(jnp.int32, row_count)
    onehot = (pivots[:, None] == row_ids[None, :]).astype(jnp.float32)
    picked = dot(onehot, scaled, 1, 1)

    def own_quarter(vectors):
        return lax.dynamic_slice_in_dim(vectors, panel_start, quarter, 1)

    def spread(stacked):
        return stacked.transpose(1, 0, 2).reshape(vec, -1)

    quarter_points, picks, rhs_parts = gather(
        [own_quarter(scaled).T, picked, own_quarter(right_sides)], "blk", 0
    )
    visit = quarter_points.reshape(-1, points.shape[0])
    visit_sq = jnp.sum(visit * visit, axis=1)
    rhs_q = spread(rhs_parts)
    (pivot_parts,) = gather([jnp.sum(picks, axis=0)], "panel", 1)
    pivot_rows = pivot_parts.reshape(-1, points.shape[0])
    pivot_sq = jnp.sum(pivot_rows * pivot_rows, axis=1)

    panel_q = kern(pivot_rows, pivot_sq, visit, 1, visit_sq)
    panel_own = kern(pivot_rows, pivot_sq, scaled, 0, local_sq)
    inner_kernel = kern(pivot_rows, pivot_sq, pivot_rows, 1, pivot_sq)
    tile = kern(visit, visit_sq, scaled, 0, local_sq)

    gram, proj = sum_over([dot(panel_q, panel_q, 1, 1), dot(rhs_q, panel_q, 1, 1)], "panel", 2)
    inverse = inverse_of(noise * inner_kernel + gram)

    def coefficients_of(projected):
        return dot(projected, inverse, 1, 0)

    def precondition(resid, coefficients, panel_rows):
        return (resid - dot(coefficients, panel_rows, 1, 0)) / noise

    coef = coefficients_of(proj)
    dir_q = precondition(rhs_q, coef, panel_q)
    dir_own = precondition(right_sides, coef, panel_own)
    (image_own,) = sum_over([dot(dir_q, tile, 1, 0)], "panel", 3)
    image_own = image_own + noise * dir_own
    (image_parts,) = gather([own_quarter(image_own)], "blk", 4)
    image_q = spread(image_parts)
    lanes = lax.broadcasted_iota(jnp.int32, (1, 128), 1)

    def pack(columns):
        packed = jnp.zeros((vec, 128), jnp.float32)
        for index, column in enumerate(columns):
            packed = jnp.where(lanes == index, column[:, None], packed)
        return packed

    image_proj, dots = sum_over(
        [
            dot(image_q, panel_q, 1, 1),
            pack([jnp.sum(rhs_q * dir_q, axis=1), jnp.sum(dir_q * image_q, axis=1)]),
        ],
        "panel",
        5,
    )
    norm, curvature = dots[:, 0], dots[:, 1]
    step = (norm / curvature)[:, None]
    coef = coefficients_of(proj - step * image_proj)
    resid_own = right_sides - step * image_own
    pre_q = precondition(rhs_q - step * image_q, coef, panel_q)
    pre_own = precondition(resid_own, coef, panel_own)
    (pre_image,) = sum_over([dot(pre_q, tile, 1, 0)], "panel", 6)
    pre_image = pre_image + noise * pre_own
    (dot_parts,) = gather(
        [
            pack(
                [
                    jnp.sum(resid_own * pre_own, axis=1),
                    jnp.sum(pre_own * pre_image, axis=1),
                    jnp.sum(pre_own * image_own + dir_own * pre_image, axis=1),
                ]
            )
        ],
        "blk",
        7,
    )
    dots = jnp.sum(dot_parts, axis=0)
    new_norm = dots[:, 0]
    ratio = new_norm / norm
    curvature = dots[:, 1] + ratio * (dots[:, 2] + ratio * curvature)
    last = (new_norm / curvature)[:, None]
    ratio = ratio[:, None]
    solution = step * dir_own + last * (pre_own + ratio * dir_own)
    residual = resid_own - last * (pre_image + ratio * image_own)
    return (solution, residual)


def solution(mesh):
    return jax.shard_map(
        per_device,
        mesh=mesh,
        in_specs=(P(None, "blk"), P(), P(), P(None, "blk"), P("panel")),
        out_specs=(P(None, "blk"), P(None, "blk")),
        check_vma=False,
    )
```

```python
import functools

import jax
import jax.numpy as jnp
from jax import lax
from jax.experimental import pallas as pl
from jax.experimental.pallas import tpu as pltpu
from jax.sharding import PartitionSpec as P

FULL = lax.Precision.HIGHEST
VMEM = pl.BlockSpec(memory_space=pltpu.VMEM)
MESH = pl.DeviceIdType.MESH
VMEM_BYTES = 16 * 1024 * 1024
LOOP_BYTES = 28 * 1024 * 1024


def dot(left, right, left_dim, right_dim, precision=lax.Precision.HIGH):
    return lax.dot_general(
        left,
        right,
        (((left_dim,), (right_dim,)), ((), ())),
        precision=precision,
        preferred_element_type=jnp.float32,
    )


def gather_kernel(axis, size, count, *refs):
    ins, outs = refs[:count], refs[count : 2 * count]
    send_sem, recv_sem = refs[2 * count :]
    me = lax.axis_index(axis)
    barrier = pltpu.get_barrier_semaphore()
    for hop in range(1, size):
        pl.semaphore_signal(
            barrier, inc=1, device_id={axis: lax.rem(me + hop, size)}, device_id_type=MESH
        )
    pl.semaphore_wait(barrier, size - 1)

    def copy_of(item, hop, slot):
        return pltpu.make_async_remote_copy(
            src_ref=ins[item],
            dst_ref=outs[item].at[slot],
            send_sem=send_sem.at[item, hop],
            recv_sem=recv_sem.at[item, hop],
            device_id={axis: lax.rem(me + hop, size)},
            device_id_type=MESH,
        )

    for hop in range(size - 1, 0, -1):
        for item in range(count):
            copy_of(item, hop, me).start()
    for item in range(count):
        outs[item][me] = ins[item][...]
    for hop in range(1, size):
        for item in range(count):
            copy_of(item, hop, lax.rem(me + size - hop, size)).wait_recv()
    for hop in range(1, size):
        for item in range(count):
            copy_of(item, hop, me).wait_send()


def gather(arrays, axis, collective_id):
    size = lax.axis_size(axis)
    count = len(arrays)
    return pl.pallas_call(
        functools.partial(gather_kernel, axis, size, count),
        out_shape=[jax.ShapeDtypeStruct((size,) + a.shape, a.dtype) for a in arrays],
        in_specs=[VMEM] * count,
        out_specs=[VMEM] * count,
        scratch_shapes=[
            pltpu.SemaphoreType.DMA((count, size)),
            pltpu.SemaphoreType.DMA((count, size)),
        ],
        compiler_params=pltpu.CompilerParams(
            collective_id=collective_id, has_side_effects=True, vmem_limit_bytes=VMEM_BYTES
        ),
    )(*arrays)


def forward_kernel(axis, size, count, *refs):
    ins, outs = refs[:count], refs[count : 2 * count]
    up_send, up_recv, down_send, down_recv, pair_send, pair_recv = refs[2 * count :]
    half = size // 2
    me = lax.axis_index(axis)
    place = me // 2
    partner = me + 1 - 2 * lax.rem(me, 2)
    has_above, has_below = place < half - 1, place > 0
    barrier = pltpu.get_barrier_semaphore()

    def greet(device):
        pl.semaphore_signal(barrier, inc=1, device_id={axis: device}, device_id_type=MESH)

    greet(partner)
    pl.when(has_above)(lambda: greet(me + 2))
    pl.when(has_below)(lambda: greet(me - 2))
    pl.semaphore_wait(barrier, 1 + has_above.astype(jnp.int32) + has_below.astype(jnp.int32))

    def copies(own, slot, sends, recvs, index, device):
        return [
            pltpu.make_async_remote_copy(
                src_ref=ins[item] if own else outs[item].at[slot],
                dst_ref=outs[item].at[slot],
                send_sem=sends.at[item, index],
                recv_sem=recvs.at[item, index],
                device_id={axis: device},
                device_id_type=MESH,
            )
            for item in range(count)
        ]

    def up(distance):
        slot = me - 2 * (distance - 1)
        return copies(distance == 1, slot, up_send, up_recv, distance, me + 2)

    def down(distance):
        slot = me + 2 * (distance - 1)
        return copies(distance == 1, slot, down_send, down_recv, distance, me - 2)

    def pair(shift):
        index = abs(shift) if shift <= 0 else half - 1 + shift
        return copies(shift == 0, me + 2 * shift, pair_send, pair_recv, index, partner)

    def start(group):
        for copy in group:
            copy.start()

    def arrived(group_of, slot, sends, recvs, index):
        for copy in copies(False, slot, sends, recvs, index, group_of):
            copy.wait_recv()

    pl.when(has_above)(lambda: start(up(1)))
    pl.when(has_below)(lambda: start(down(1)))
    start(pair(0))
    for item in range(count):
        outs[item][me] = ins[item][...]
    for distance in range(1, half):

        @pl.when(place - distance >= 0)
        def _():
            arrived(partner, me - 2 * distance, up_send, up_recv, distance)
            if distance < half - 1:
                pl.when(has_above)(lambda: start(up(distance + 1)))
            start(pair(-distance))

        @pl.when(place + distance <= half - 1)
        def _():
            arrived(partner, me + 2 * distance, down_send, down_recv, distance)
            if distance < half - 1:
                pl.when(has_below)(lambda: start(down(distance + 1)))
            start(pair(distance))

    def sent(group):
        for copy in group:
            copy.wait_send()

    def settle(shift):
        index = abs(shift) if shift <= 0 else half - 1 + shift
        arrived(partner, partner + 2 * shift, pair_send, pair_recv, index)
        sent(pair(shift))

    settle(0)
    pl.when(has_above)(lambda: sent(up(1)))
    pl.when(has_below)(lambda: sent(down(1)))
    for distance in range(1, half):

        @pl.when(place - distance >= 0)
        def _():
            settle(-distance)
            if distance < half - 1:
                pl.when(has_above)(lambda: sent(up(distance + 1)))

        @pl.when(place + distance <= half - 1)
        def _():
            settle(distance)
            if distance < half - 1:
                pl.when(has_below)(lambda: sent(down(distance + 1)))


def forward_gather(arrays, axis, collective_id):
    size = lax.axis_size(axis)
    count = len(arrays)
    return pl.pallas_call(
        functools.partial(forward_kernel, axis, size, count),
        out_shape=[jax.ShapeDtypeStruct((size,) + a.shape, a.dtype) for a in arrays],
        in_specs=[VMEM] * count,
        out_specs=[VMEM] * count,
        scratch_shapes=[pltpu.SemaphoreType.DMA((count, size))] * 6,
        compiler_params=pltpu.CompilerParams(
            collective_id=collective_id, has_side_effects=True, vmem_limit_bytes=VMEM_BYTES
        ),
    )(*arrays)


def sum_kernel(axis, steps, count, *refs):
    ins, outs = refs[:count], refs[count : 2 * count]
    landed = refs[2 * count : 3 * count]
    send_sem, recv_sem = refs[3 * count :]
    me = lax.axis_index(axis)
    partners = [me + s * (1 - 2 * lax.rem(me // s, 2)) for s in steps]
    barrier = pltpu.get_barrier_semaphore()
    for partner in partners:
        pl.semaphore_signal(barrier, inc=1, device_id={axis: partner}, device_id_type=MESH)
    pl.semaphore_wait(barrier, len(steps))
    held = list(ins)
    for step, partner in enumerate(partners):
        copies = []
        for item in range(count):
            copy = pltpu.make_async_remote_copy(
                src_ref=held[item],
                dst_ref=landed[item].at[step],
                send_sem=send_sem.at[item, step],
                recv_sem=recv_sem.at[item, step],
                device_id={axis: partner},
                device_id_type=MESH,
            )
            copy.start()
            copies.append(copy)
        for item in range(count):
            copies[item].wait()
            outs[item][...] = held[item][...] + landed[item][step]
            held[item] = outs[item]


def sum_over(arrays, axis, collective_id):
    size = lax.axis_size(axis)
    steps = []
    while (1 << len(steps)) < size:
        steps.append(1 << len(steps))
    count = len(arrays)
    return pl.pallas_call(
        functools.partial(sum_kernel, axis, steps, count),
        out_shape=[jax.ShapeDtypeStruct(a.shape, a.dtype) for a in arrays],
        in_specs=[VMEM] * count,
        out_specs=[VMEM] * count,
        scratch_shapes=[pltpu.VMEM((len(steps),) + a.shape, a.dtype) for a in arrays]
        + [
            pltpu.SemaphoreType.DMA((count, len(steps))),
            pltpu.SemaphoreType.DMA((count, len(steps))),
        ],
        compiler_params=pltpu.CompilerParams(
            collective_id=collective_id, has_side_effects=True, vmem_limit_bytes=VMEM_BYTES
        ),
    )(*arrays)


def inverse_kernel(side, part, width, a_ref, out_ref):
    sub = lax.broadcasted_iota(jnp.int32, (part, part), 0)
    lane = lax.broadcasted_iota(jnp.int32, (part, part), 1)
    head = lax.broadcasted_iota(jnp.int32, (1, part), 1)
    out_ref[...] = a_ref[...]

    def block_step(_, carry):
        block = out_ref[:part, :part]
        for first in range(0, part, width):
            columns = [
                jnp.broadcast_to(block[:, k : k + 1], (part, part))
                for k in range(first, first + width)
            ]
            for index in range(width):
                k = first + index
                here = sub == k
                column = columns[index]
                scale = 1.0 / column[k : k + 1, :]
                row = jnp.where(head == k, 1.0, block[k : k + 1, :]) * scale
                factor = jnp.where(here, -1.0, column)
                block = jnp.where(here | (lane == k), 0.0, block) - factor * row
                for later in range(index + 1, width):
                    entry = columns[later][k : k + 1, :] * scale
                    columns[later] = jnp.where(here, 0.0, columns[later]) - factor * entry
        left = out_ref[part:, :part]
        right = dot(block, out_ref[:part, part:], 1, 0, FULL)
        rest = out_ref[part:, part:] - dot(left, right, 1, 0, FULL)
        side_part = -dot(left, block, 1, 0, FULL)
        out_ref[...] = jnp.concatenate(
            [
                jnp.concatenate([rest, side_part], axis=1),
                jnp.concatenate([right, block], axis=1),
            ],
            axis=0,
        )
        return carry

    lax.fori_loop(0, side // part, block_step, 0)


def inverse_of(matrix):
    side = matrix.shape[0]
    return pl.pallas_call(
        functools.partial(inverse_kernel, side, 64, 8),
        out_shape=jax.ShapeDtypeStruct(matrix.shape, matrix.dtype),
        in_specs=[VMEM],
        out_specs=VMEM,
        compiler_params=pltpu.CompilerParams(vmem_limit_bytes=VMEM_BYTES),
    )(matrix)


def kern(left, left_sq, right, right_dim, right_sq):
    cross = dot(left, right, 1, right_dim, FULL)
    return jnp.exp(-0.5 * (left_sq[:, None] + right_sq[None, :] - 2.0 * cross))


def loop_kernel(size, panel_size, vec, quarter, *refs):
    proj_ref, inverse_ref, rhs_parts, rhs_own, panel_parts, panel_own = refs[:6]
    high_ref, low_ref, noise_ref, solution_ref, residual_ref = refs[6:11]
    dir_parts, pre_parts, first_sum, second_sum, image_parts, dot_sum, last_sum = refs[11:18]
    send_sem, recv_sem = refs[18:]
    row, column = lax.axis_index("blk"), lax.axis_index("panel")
    rank = proj_ref.shape[1]
    barrier = pltpu.get_barrier_semaphore()
    for hop in range(1, size):
        pl.semaphore_signal(
            barrier, inc=1, device_id={"blk": lax.rem(row + hop, size)}, device_id_type=MESH
        )
    for hop in range(1, panel_size):
        pl.semaphore_signal(
            barrier,
            inc=1,
            device_id={"panel": lax.rem(column + hop, panel_size)},
            device_id_type=MESH,
        )
    noise = noise_ref[...]

    def exchange(axis, buffer, phase):
        me, count = (row, size) if axis == "blk" else (column, panel_size)

        def copy_of(hop, slot):
            return pltpu.make_async_remote_copy(
                src_ref=buffer.at[slot],
                dst_ref=buffer.at[slot],
                send_sem=send_sem.at[phase, hop],
                recv_sem=recv_sem.at[phase, hop],
                device_id={axis: lax.rem(me + hop, count)},
                device_id_type=MESH,
            )

        for hop in range(count - 1, 0, -1):
            copy_of(hop, me).start()
        for hop in range(1, count):
            copy_of(hop, lax.rem(me + count - hop, count)).wait_recv()
        for hop in range(1, count):
            copy_of(hop, me).wait_send()

    def total_of(buffer, count):
        total = buffer[0]
        for index in range(1, count):
            total = total + buffer[index]
        return total

    def precondition(resid, coefficients, panel_rows):
        return (resid - dot(coefficients, panel_rows, 1, 0, FULL)) / noise

    def tile_product(parts):
        product = jnp.zeros(rhs_own.shape, jnp.float32)
        for index in range(size):
            rows = pl.ds(index * quarter, quarter)
            part = parts[index]
            high = part.astype(jnp.bfloat16)
            low = (part - high.astype(jnp.float32)).astype(jnp.bfloat16)
            for left, right in ((high, high_ref), (low, high_ref), (high, low_ref)):
                product = product + lax.dot_general(
                    left,
                    right[rows, :],
                    (((1,), (0,)), ((), ())),
                    preferred_element_type=jnp.float32,
                )
        return product

    def row_sum(left, right):
        return jnp.sum(left * right, axis=1, keepdims=True)

    lanes = lax.broadcasted_iota(jnp.int32, (vec, 128), 1)

    def pack(columns):
        packed = jnp.zeros((vec, 128), jnp.float32)
        for index, value in enumerate(columns):
            packed = jnp.where(lanes == index, value, packed)
        return packed

    coef = dot(proj_ref[...], inverse_ref[...], 1, 0, FULL)
    for index in range(size):
        dir_parts[index] = precondition(rhs_parts[index], coef, panel_parts[index])
    first_sum[column] = tile_product(dir_parts)
    pl.semaphore_wait(barrier, size + panel_size - 2)
    exchange("panel", first_sum, 0)
    dir_own = precondition(rhs_own[...], coef, panel_own[...])
    image_own = total_of(first_sum, panel_size) + noise * dir_own
    for index in range(panel_size):

        @pl.when(column == index)
        def _():
            image_parts[row] = image_own[:, index * quarter : (index + 1) * quarter]

    exchange("blk", image_parts, 1)
    image_proj = jnp.zeros((vec, rank), jnp.float32)
    norm = jnp.zeros((vec, 1), jnp.float32)
    curvature = jnp.zeros((vec, 1), jnp.float32)
    for index in range(size):
        image_proj = image_proj + dot(image_parts[index], panel_parts[index], 1, 1, FULL)
        norm = norm + row_sum(rhs_parts[index], dir_parts[index])
        curvature = curvature + row_sum(dir_parts[index], image_parts[index])
    dot_sum[column, :, :rank] = image_proj
    dot_sum[column, :, rank:] = pack([norm, curvature])
    exchange("panel", dot_sum, 2)
    totals = total_of(dot_sum, panel_size)
    image_proj = totals[:, :rank]
    norm, curvature = totals[:, rank : rank + 1], totals[:, rank + 1 : rank + 2]
    step = norm / curvature
    coef = dot(proj_ref[...] - step * image_proj, inverse_ref[...], 1, 0, FULL)
    for index in range(size):
        pre_parts[index] = precondition(
            rhs_parts[index] - step * image_parts[index], coef, panel_parts[index]
        )
    second_sum[column] = tile_product(pre_parts)
    exchange("panel", second_sum, 3)
    resid_own = rhs_own[...] - step * image_own
    pre_own = precondition(resid_own, coef, panel_own[...])
    pre_image = total_of(second_sum, panel_size) + noise * pre_own
    last_sum[row] = pack(
        [
            row_sum(resid_own, pre_own),
            row_sum(pre_own, pre_image),
            row_sum(pre_own, image_own) + row_sum(dir_own, pre_image),
        ]
    )
    exchange("blk", last_sum, 4)
    totals = total_of(last_sum, size)
    new_norm = totals[:, 0:1]
    ratio = new_norm / norm
    curvature = totals[:, 1:2] + ratio * (totals[:, 2:3] + ratio * curvature)
    last = new_norm / curvature
    solution_ref[...] = step * dir_own + last * (pre_own + ratio * dir_own)
    residual_ref[...] = resid_own - last * (pre_image + ratio * image_own)


def loop_of(proj, inverse, rhs_parts, rhs_own, panel_parts, panel_own, tile, noise):
    size, vec, quarter = rhs_parts.shape
    panel_size = lax.axis_size("panel")
    rank = proj.shape[1]
    rounded = lax.reduce_precision(tile, 8, 7)
    high = rounded.astype(jnp.bfloat16)
    low = (tile - rounded).astype(jnp.bfloat16)
    most = max(size, panel_size)
    own = jax.ShapeDtypeStruct(rhs_own.shape, jnp.float32)
    return pl.pallas_call(
        functools.partial(loop_kernel, size, panel_size, vec, quarter),
        out_shape=[own, own],
        in_specs=[VMEM] * 9,
        out_specs=[VMEM] * 2,
        scratch_shapes=[
            pltpu.VMEM(rhs_parts.shape, jnp.float32),
            pltpu.VMEM(rhs_parts.shape, jnp.float32),
            pltpu.VMEM((panel_size,) + rhs_own.shape, jnp.float32),
            pltpu.VMEM((panel_size,) + rhs_own.shape, jnp.float32),
            pltpu.VMEM(rhs_parts.shape, jnp.float32),
            pltpu.VMEM((panel_size, vec, rank + 128), jnp.float32),
            pltpu.VMEM((size, vec, 128), jnp.float32),
            pltpu.SemaphoreType.DMA((5, most)),
            pltpu.SemaphoreType.DMA((5, most)),
        ],
        compiler_params=pltpu.CompilerParams(
            collective_id=8, has_side_effects=True, vmem_limit_bytes=LOOP_BYTES
        ),
    )(proj, inverse, rhs_parts, rhs_own, panel_parts, panel_own, high, low, noise)


def per_device(points, lengthscale, noise_level, right_sides, pivots):
    row_count = points.shape[1]
    vec = right_sides.shape[0]
    panel_size = lax.axis_size("panel")
    quarter = row_count // panel_size
    panel_start = lax.axis_index("panel") * quarter
    noise = noise_level[0]
    scaled = points / lengthscale[:, None]
    local_sq = jnp.sum(scaled * scaled, axis=0)
    row_ids = lax.axis_index("blk") * row_count + lax.iota(jnp.int32, row_count)
    onehot = (pivots[:, None] == row_ids[None, :]).astype(jnp.float32)
    picked = dot(onehot, scaled, 1, 1, FULL)

    def own_quarter(vectors):
        return lax.dynamic_slice_in_dim(vectors, panel_start, quarter, 1)

    def spread(stacked):
        return stacked.transpose(1, 0, 2).reshape(vec, -1)

    quarter_points, picks, rhs_parts = forward_gather(
        [own_quarter(scaled).T, picked, own_quarter(right_sides)], "blk", 0
    )
    visit = quarter_points.reshape(-1, points.shape[0])
    visit_sq = jnp.sum(visit * visit, axis=1)
    rhs_q = spread(rhs_parts)
    (pivot_parts,) = gather([jnp.sum(picks, axis=0)], "panel", 1)
    pivot_rows = pivot_parts.reshape(-1, points.shape[0])
    pivot_sq = jnp.sum(pivot_rows * pivot_rows, axis=1)

    panel_q = kern(pivot_rows, pivot_sq, visit, 1, visit_sq)
    panel_own = kern(pivot_rows, pivot_sq, scaled, 0, local_sq)
    inner_kernel = kern(pivot_rows, pivot_sq, pivot_rows, 1, pivot_sq)
    tile = kern(visit, visit_sq, scaled, 0, local_sq)

    gram, proj = sum_over([dot(panel_q, panel_q, 1, 1), dot(rhs_q, panel_q, 1, 1)], "panel", 2)
    inverse = inverse_of(noise * inner_kernel + gram)

    if 4 * tile.size <= LOOP_BYTES // 3:
        blocks = panel_q.reshape(panel_q.shape[0], -1, quarter).transpose(1, 0, 2)
        return tuple(
            loop_of(
                proj, inverse, rhs_parts, right_sides, blocks, panel_own, tile,
                noise_level.reshape(1, 1),
            )
        )

    def coefficients_of(projected):
        return dot(projected, inverse, 1, 0, FULL)

    def precondition(resid, coefficients, panel_rows):
        return (resid - dot(coefficients, panel_rows, 1, 0)) / noise

    coef = coefficients_of(proj)
    dir_q = precondition(rhs_q, coef, panel_q)
    dir_own = precondition(right_sides, coef, panel_own)
    (image_own,) = sum_over([dot(dir_q, tile, 1, 0)], "panel", 3)
    image_own = image_own + noise * dir_own
    (image_parts,) = gather([own_quarter(image_own)], "blk", 4)
    image_q = spread(image_parts)
    lanes = lax.broadcasted_iota(jnp.int32, (1, 128), 1)

    def pack(columns):
        packed = jnp.zeros((vec, 128), jnp.float32)
        for index, column in enumerate(columns):
            packed = jnp.where(lanes == index, column[:, None], packed)
        return packed

    image_proj, dots = sum_over(
        [
            dot(image_q, panel_q, 1, 1),
            pack([jnp.sum(rhs_q * dir_q, axis=1), jnp.sum(dir_q * image_q, axis=1)]),
        ],
        "panel",
        5,
    )
    norm, curvature = dots[:, 0], dots[:, 1]
    step = (norm / curvature)[:, None]
    coef = coefficients_of(proj - step * image_proj)
    resid_own = right_sides - step * image_own
    pre_q = precondition(rhs_q - step * image_q, coef, panel_q)
    pre_own = precondition(resid_own, coef, panel_own)
    (pre_image,) = sum_over([dot(pre_q, tile, 1, 0)], "panel", 6)
    pre_image = pre_image + noise * pre_own
    (dot_parts,) = gather(
        [
            pack(
                [
                    jnp.sum(resid_own * pre_own, axis=1),
                    jnp.sum(pre_own * pre_image, axis=1),
                    jnp.sum(pre_own * image_own + dir_own * pre_image, axis=1),
                ]
            )
        ],
        "blk",
        7,
    )
    dots = jnp.sum(dot_parts, axis=0)
    new_norm = dots[:, 0]
    ratio = new_norm / norm
    curvature = dots[:, 1] + ratio * (dots[:, 2] + ratio * curvature)
    last = (new_norm / curvature)[:, None]
    ratio = ratio[:, None]
    solution = step * dir_own + last * (pre_own + ratio * dir_own)
    residual = resid_own - last * (pre_image + ratio * image_own)
    return (solution, residual)


def solution(mesh):
    return jax.shard_map(
        per_device,
        mesh=mesh,
        in_specs=(P(None, "blk"), P(), P(), P(None, "blk"), P("panel")),
        out_specs=(P(None, "blk"), P(None, "blk")),
        check_vma=False,
    )
```

```python
import functools

import jax
import jax.numpy as jnp
from jax import lax
from jax.experimental import pallas as pl
from jax.experimental.pallas import tpu as pltpu
from jax.sharding import PartitionSpec as P

FULL = lax.Precision.HIGHEST
VMEM = pl.BlockSpec(memory_space=pltpu.VMEM)
MESH = pl.DeviceIdType.MESH
VMEM_BYTES = 16 * 1024 * 1024
LOOP_BYTES = 28 * 1024 * 1024


def dot(left, right, left_dim, right_dim, precision=lax.Precision.HIGH):
    return lax.dot_general(
        left,
        right,
        (((left_dim,), (right_dim,)), ((), ())),
        precision=precision,
        preferred_element_type=jnp.float32,
    )


def gather_kernel(axis, size, count, *refs):
    ins, outs = refs[:count], refs[count : 2 * count]
    send_sem, recv_sem = refs[2 * count :]
    me = lax.axis_index(axis)
    barrier = pltpu.get_barrier_semaphore()
    for hop in range(1, size):
        pl.semaphore_signal(
            barrier, inc=1, device_id={axis: lax.rem(me + hop, size)}, device_id_type=MESH
        )
    pl.semaphore_wait(barrier, size - 1)

    def copy_of(item, hop, slot):
        return pltpu.make_async_remote_copy(
            src_ref=ins[item],
            dst_ref=outs[item].at[slot],
            send_sem=send_sem.at[item, hop],
            recv_sem=recv_sem.at[item, hop],
            device_id={axis: lax.rem(me + hop, size)},
            device_id_type=MESH,
        )

    for hop in range(size - 1, 0, -1):
        for item in range(count):
            copy_of(item, hop, me).start()
    for item in range(count):
        outs[item][me] = ins[item][...]
    for hop in range(1, size):
        for item in range(count):
            copy_of(item, hop, lax.rem(me + size - hop, size)).wait_recv()
    for hop in range(1, size):
        for item in range(count):
            copy_of(item, hop, me).wait_send()


def gather(arrays, axis, collective_id):
    size = lax.axis_size(axis)
    count = len(arrays)
    return pl.pallas_call(
        functools.partial(gather_kernel, axis, size, count),
        out_shape=[jax.ShapeDtypeStruct((size,) + a.shape, a.dtype) for a in arrays],
        in_specs=[VMEM] * count,
        out_specs=[VMEM] * count,
        scratch_shapes=[
            pltpu.SemaphoreType.DMA((count, size)),
            pltpu.SemaphoreType.DMA((count, size)),
        ],
        compiler_params=pltpu.CompilerParams(
            collective_id=collective_id, has_side_effects=True, vmem_limit_bytes=VMEM_BYTES
        ),
    )(*arrays)


def forward_kernel(axis, size, count, *refs):
    ins, outs = refs[:count], refs[count : 2 * count]
    up_send, up_recv, down_send, down_recv, pair_send, pair_recv = refs[2 * count :]
    half = size // 2
    me = lax.axis_index(axis)
    place = me // 2
    partner = me + 1 - 2 * lax.rem(me, 2)
    has_above, has_below = place < half - 1, place > 0
    barrier = pltpu.get_barrier_semaphore()

    def greet(device):
        pl.semaphore_signal(barrier, inc=1, device_id={axis: device}, device_id_type=MESH)

    greet(partner)
    pl.when(has_above)(lambda: greet(me + 2))
    pl.when(has_below)(lambda: greet(me - 2))
    pl.semaphore_wait(barrier, 1 + has_above.astype(jnp.int32) + has_below.astype(jnp.int32))

    def copies(own, slot, sends, recvs, index, device):
        return [
            pltpu.make_async_remote_copy(
                src_ref=ins[item] if own else outs[item].at[slot],
                dst_ref=outs[item].at[slot],
                send_sem=sends.at[item, index],
                recv_sem=recvs.at[item, index],
                device_id={axis: device},
                device_id_type=MESH,
            )
            for item in range(count)
        ]

    def up(distance):
        slot = me - 2 * (distance - 1)
        return copies(distance == 1, slot, up_send, up_recv, distance, me + 2)

    def down(distance):
        slot = me + 2 * (distance - 1)
        return copies(distance == 1, slot, down_send, down_recv, distance, me - 2)

    def pair(shift):
        index = abs(shift) if shift <= 0 else half - 1 + shift
        return copies(shift == 0, me + 2 * shift, pair_send, pair_recv, index, partner)

    def start(group):
        for copy in group:
            copy.start()

    def arrived(group_of, slot, sends, recvs, index):
        for copy in copies(False, slot, sends, recvs, index, group_of):
            copy.wait_recv()

    pl.when(has_above)(lambda: start(up(1)))
    pl.when(has_below)(lambda: start(down(1)))
    start(pair(0))
    for item in range(count):
        outs[item][me] = ins[item][...]
    for distance in range(1, half):

        @pl.when(place - distance >= 0)
        def _():
            arrived(partner, me - 2 * distance, up_send, up_recv, distance)
            if distance < half - 1:
                pl.when(has_above)(lambda: start(up(distance + 1)))
            start(pair(-distance))

        @pl.when(place + distance <= half - 1)
        def _():
            arrived(partner, me + 2 * distance, down_send, down_recv, distance)
            if distance < half - 1:
                pl.when(has_below)(lambda: start(down(distance + 1)))
            start(pair(distance))

    def sent(group):
        for copy in group:
            copy.wait_send()

    def settle(shift):
        index = abs(shift) if shift <= 0 else half - 1 + shift
        arrived(partner, partner + 2 * shift, pair_send, pair_recv, index)
        sent(pair(shift))

    settle(0)
    pl.when(has_above)(lambda: sent(up(1)))
    pl.when(has_below)(lambda: sent(down(1)))
    for distance in range(1, half):

        @pl.when(place - distance >= 0)
        def _():
            settle(-distance)
            if distance < half - 1:
                pl.when(has_above)(lambda: sent(up(distance + 1)))

        @pl.when(place + distance <= half - 1)
        def _():
            settle(distance)
            if distance < half - 1:
                pl.when(has_below)(lambda: sent(down(distance + 1)))


def forward_gather(arrays, axis, collective_id):
    size = lax.axis_size(axis)
    count = len(arrays)
    return pl.pallas_call(
        functools.partial(forward_kernel, axis, size, count),
        out_shape=[jax.ShapeDtypeStruct((size,) + a.shape, a.dtype) for a in arrays],
        in_specs=[VMEM] * count,
        out_specs=[VMEM] * count,
        scratch_shapes=[pltpu.SemaphoreType.DMA((count, size))] * 6,
        compiler_params=pltpu.CompilerParams(
            collective_id=collective_id, has_side_effects=True, vmem_limit_bytes=VMEM_BYTES
        ),
    )(*arrays)


def tile_rows(refs, first, last, chunk):
    visit_ref, scaled_ref, sq_ref, high_ref, low_ref = refs

    def one(index, carry):
        rows = pl.ds(pl.multiple_of(index * chunk, 16), chunk)
        left = visit_ref[rows, :]
        cross = dot(left, scaled_ref[...], 1, 0, FULL)
        left_sq = jnp.sum(left * left, axis=1, keepdims=True)
        values = jnp.exp(-0.5 * (left_sq + sq_ref[...] - 2.0 * cross))
        high = values.astype(jnp.bfloat16)
        high_ref[rows, :] = high
        low_ref[rows, :] = (values - high.astype(jnp.float32)).astype(jnp.bfloat16)
        return carry

    lax.fori_loop(first, last, one, 0)


def sum_kernel(axis, steps, count, chunk, *refs):
    extra = 3 if chunk else 0
    ins, outs = refs[:count], refs[count + extra : 2 * count + extra]
    made = 2 * count + extra
    tile_refs = refs[count : count + extra] + refs[made : made + (2 if chunk else 0)]
    refs = refs[made + (2 if chunk else 0) :]
    landed = refs[:count]
    send_sem, recv_sem = refs[count:]
    me = lax.axis_index(axis)
    partners = [me + s * (1 - 2 * lax.rem(me // s, 2)) for s in steps]
    barrier = pltpu.get_barrier_semaphore()
    for partner in partners:
        pl.semaphore_signal(barrier, inc=1, device_id={axis: partner}, device_id_type=MESH)
    pl.semaphore_wait(barrier, len(steps))
    held = list(ins)
    for step, partner in enumerate(partners):
        copies = []
        for item in range(count):
            copy = pltpu.make_async_remote_copy(
                src_ref=held[item],
                dst_ref=landed[item].at[step],
                send_sem=send_sem.at[item, step],
                recv_sem=recv_sem.at[item, step],
                device_id={axis: partner},
                device_id_type=MESH,
            )
            copy.start()
            copies.append(copy)
        if chunk:
            pieces = tile_refs[0].shape[0] // chunk
            cut = [pieces * (step + i) // len(steps) for i in (0, 1)]
            tile_rows(tile_refs, cut[0], cut[1], chunk)
        for item in range(count):
            copies[item].wait()
            outs[item][...] = held[item][...] + landed[item][step]
            held[item] = outs[item]


def sum_over(arrays, axis, collective_id, tile_of=(), chunk=0):
    size = lax.axis_size(axis)
    steps = []
    while (1 << len(steps)) < size:
        steps.append(1 << len(steps))
    count = len(arrays)
    halves = []
    if chunk:
        shape = (tile_of[0].shape[0], tile_of[1].shape[1])
        halves = [jax.ShapeDtypeStruct(shape, jnp.bfloat16)] * 2
    return pl.pallas_call(
        functools.partial(sum_kernel, axis, steps, count, chunk),
        out_shape=[jax.ShapeDtypeStruct(a.shape, a.dtype) for a in arrays] + halves,
        in_specs=[VMEM] * (count + len(tile_of)),
        out_specs=[VMEM] * (count + len(halves)),
        scratch_shapes=[pltpu.VMEM((len(steps),) + a.shape, a.dtype) for a in arrays]
        + [
            pltpu.SemaphoreType.DMA((count, len(steps))),
            pltpu.SemaphoreType.DMA((count, len(steps))),
        ],
        compiler_params=pltpu.CompilerParams(
            collective_id=collective_id, has_side_effects=True, vmem_limit_bytes=VMEM_BYTES
        ),
    )(*arrays, *tile_of)


def inverse_kernel(side, part, width, a_ref, out_ref):
    sub = lax.broadcasted_iota(jnp.int32, (part, part), 0)
    lane = lax.broadcasted_iota(jnp.int32, (part, part), 1)
    head = lax.broadcasted_iota(jnp.int32, (1, part), 1)
    out_ref[...] = a_ref[...]

    def block_step(_, carry):
        block = out_ref[:part, :part]
        for first in range(0, part, width):
            columns = [
                jnp.broadcast_to(block[:, k : k + 1], (part, part))
                for k in range(first, first + width)
            ]
            for index in range(width):
                k = first + index
                here = sub == k
                column = columns[index]
                scale = 1.0 / column[k : k + 1, :]
                row = jnp.where(head == k, 1.0, block[k : k + 1, :]) * scale
                factor = jnp.where(here, -1.0, column)
                block = jnp.where(here | (lane == k), 0.0, block) - factor * row
                for later in range(index + 1, width):
                    entry = columns[later][k : k + 1, :] * scale
                    columns[later] = jnp.where(here, 0.0, columns[later]) - factor * entry
        left = out_ref[part:, :part]
        right = dot(block, out_ref[:part, part:], 1, 0, FULL)
        rest = out_ref[part:, part:] - dot(left, right, 1, 0, FULL)
        side_part = -dot(left, block, 1, 0, FULL)
        out_ref[...] = jnp.concatenate(
            [
                jnp.concatenate([rest, side_part], axis=1),
                jnp.concatenate([right, block], axis=1),
            ],
            axis=0,
        )
        return carry

    lax.fori_loop(0, side // part, block_step, 0)


def inverse_of(matrix):
    side = matrix.shape[0]
    return pl.pallas_call(
        functools.partial(inverse_kernel, side, 64, 8),
        out_shape=jax.ShapeDtypeStruct(matrix.shape, matrix.dtype),
        in_specs=[VMEM],
        out_specs=VMEM,
        compiler_params=pltpu.CompilerParams(vmem_limit_bytes=VMEM_BYTES),
    )(matrix)


def kern(left, left_sq, right, right_dim, right_sq):
    cross = dot(left, right, 1, right_dim, FULL)
    return jnp.exp(-0.5 * (left_sq[:, None] + right_sq[None, :] - 2.0 * cross))


def loop_kernel(size, panel_size, vec, quarter, *refs):
    proj_ref, inverse_ref, rhs_visit, rhs_own, panel_visit, panel_own = refs[:6]
    high_ref, low_ref, noise_ref, solution_ref, residual_ref = refs[6:11]
    first_sum, second_sum, image_parts, dot_sum, last_sum = refs[11:16]
    send_sem, recv_sem = refs[16:]
    row, column = lax.axis_index("blk"), lax.axis_index("panel")
    rank = proj_ref.shape[1]
    barrier = pltpu.get_barrier_semaphore()
    for hop in range(1, size):
        pl.semaphore_signal(
            barrier, inc=1, device_id={"blk": lax.rem(row + hop, size)}, device_id_type=MESH
        )
    for hop in range(1, panel_size):
        pl.semaphore_signal(
            barrier,
            inc=1,
            device_id={"panel": lax.rem(column + hop, panel_size)},
            device_id_type=MESH,
        )
    noise = noise_ref[...]

    def exchange(axis, buffer, phase):
        me, count = (row, size) if axis == "blk" else (column, panel_size)

        def copy_of(hop, slot):
            return pltpu.make_async_remote_copy(
                src_ref=buffer.at[slot],
                dst_ref=buffer.at[slot],
                send_sem=send_sem.at[phase, hop],
                recv_sem=recv_sem.at[phase, hop],
                device_id={axis: lax.rem(me + hop, count)},
                device_id_type=MESH,
            )

        for hop in range(count - 1, 0, -1):
            copy_of(hop, me).start()
        for hop in range(1, count):
            copy_of(hop, lax.rem(me + count - hop, count)).wait_recv()
        for hop in range(1, count):
            copy_of(hop, me).wait_send()

    def total_of(buffer, count):
        total = buffer[0]
        for index in range(1, count):
            total = total + buffer[index]
        return total

    def precondition(resid, coefficients, panel_rows):
        return (resid - dot(coefficients, panel_rows, 1, 0, FULL)) / noise

    def tile_product(vectors):
        high = vectors.astype(jnp.bfloat16)
        low = (vectors - high.astype(jnp.float32)).astype(jnp.bfloat16)
        product = jnp.zeros(rhs_own.shape, jnp.float32)
        for left, right in ((high, high_ref), (low, high_ref), (high, low_ref)):
            product = product + lax.dot_general(
                left,
                right[...],
                (((1,), (0,)), ((), ())),
                preferred_element_type=jnp.float32,
            )
        return product

    def row_sum(left, right):
        return jnp.sum(left * right, axis=1, keepdims=True)

    lanes = lax.broadcasted_iota(jnp.int32, (vec, 128), 1)

    def pack(columns):
        packed = jnp.zeros((vec, 128), jnp.float32)
        for index, value in enumerate(columns):
            packed = jnp.where(lanes == index, value, packed)
        return packed

    coef = dot(proj_ref[...], inverse_ref[...], 1, 0, FULL)
    dir_visit = precondition(rhs_visit[...], coef, panel_visit[...])
    first_sum[column] = tile_product(dir_visit)
    pl.semaphore_wait(barrier, size + panel_size - 2)
    exchange("panel", first_sum, 0)
    dir_own = precondition(rhs_own[...], coef, panel_own[...])
    image_own = total_of(first_sum, panel_size) + noise * dir_own
    for index in range(panel_size):

        @pl.when(column == index)
        def _():
            image_parts[row] = image_own[:, index * quarter : (index + 1) * quarter]

    exchange("blk", image_parts, 1)
    image_visit = jnp.concatenate([image_parts[index] for index in range(size)], axis=1)
    image_proj = dot(image_visit, panel_visit[...], 1, 1, FULL)
    norm = row_sum(rhs_visit[...], dir_visit)
    curvature = row_sum(dir_visit, image_visit)
    dot_sum[column, :, :rank] = image_proj
    dot_sum[column, :, rank:] = pack([norm, curvature])
    exchange("panel", dot_sum, 2)
    totals = total_of(dot_sum, panel_size)
    image_proj = totals[:, :rank]
    norm, curvature = totals[:, rank : rank + 1], totals[:, rank + 1 : rank + 2]
    step = norm / curvature
    coef = dot(proj_ref[...] - step * image_proj, inverse_ref[...], 1, 0, FULL)
    pre_visit = precondition(rhs_visit[...] - step * image_visit, coef, panel_visit[...])
    second_sum[column] = tile_product(pre_visit)
    exchange("panel", second_sum, 3)
    resid_own = rhs_own[...] - step * image_own
    pre_own = precondition(resid_own, coef, panel_own[...])
    pre_image = total_of(second_sum, panel_size) + noise * pre_own
    last_sum[row] = pack(
        [
            row_sum(resid_own, pre_own),
            row_sum(pre_own, pre_image),
            row_sum(pre_own, image_own) + row_sum(dir_own, pre_image),
        ]
    )
    exchange("blk", last_sum, 4)
    totals = total_of(last_sum, size)
    new_norm = totals[:, 0:1]
    ratio = new_norm / norm
    curvature = totals[:, 1:2] + ratio * (totals[:, 2:3] + ratio * curvature)
    last = new_norm / curvature
    solution_ref[...] = step * dir_own + last * (pre_own + ratio * dir_own)
    residual_ref[...] = resid_own - last * (pre_image + ratio * image_own)


def loop_of(proj, inverse, rhs_visit, rhs_own, panel_visit, panel_own, high, low, noise):
    size, panel_size = lax.axis_size("blk"), lax.axis_size("panel")
    vec, rank = proj.shape
    quarter = rhs_visit.shape[1] // size
    most = max(size, panel_size)
    own = jax.ShapeDtypeStruct(rhs_own.shape, jnp.float32)
    return pl.pallas_call(
        functools.partial(loop_kernel, size, panel_size, vec, quarter),
        out_shape=[own, own],
        in_specs=[VMEM] * 9,
        out_specs=[VMEM] * 2,
        scratch_shapes=[
            pltpu.VMEM((panel_size,) + rhs_own.shape, jnp.float32),
            pltpu.VMEM((panel_size,) + rhs_own.shape, jnp.float32),
            pltpu.VMEM((size, vec, quarter), jnp.float32),
            pltpu.VMEM((panel_size, vec, rank + 128), jnp.float32),
            pltpu.VMEM((size, vec, 128), jnp.float32),
            pltpu.SemaphoreType.DMA((5, most)),
            pltpu.SemaphoreType.DMA((5, most)),
        ],
        compiler_params=pltpu.CompilerParams(
            collective_id=8, has_side_effects=True, vmem_limit_bytes=LOOP_BYTES
        ),
    )(proj, inverse, rhs_visit, rhs_own, panel_visit, panel_own, high, low, noise)


def per_device(points, lengthscale, noise_level, right_sides, pivots):
    row_count = points.shape[1]
    vec = right_sides.shape[0]
    panel_size = lax.axis_size("panel")
    quarter = row_count // panel_size
    panel_start = lax.axis_index("panel") * quarter
    noise = noise_level[0]
    scaled = points / lengthscale[:, None]
    local_sq = jnp.sum(scaled * scaled, axis=0)
    row_ids = lax.axis_index("blk") * row_count + lax.iota(jnp.int32, row_count)
    onehot = (pivots[:, None] == row_ids[None, :]).astype(jnp.float32)
    picked = dot(onehot, scaled, 1, 1, FULL)

    def own_quarter(vectors):
        return lax.dynamic_slice_in_dim(vectors, panel_start, quarter, 1)

    def spread(stacked):
        return stacked.transpose(1, 0, 2).reshape(vec, -1)

    quarter_points, picks, rhs_parts = forward_gather(
        [own_quarter(scaled).T, picked, own_quarter(right_sides)], "blk", 0
    )
    visit = quarter_points.reshape(-1, points.shape[0])
    visit_sq = jnp.sum(visit * visit, axis=1)
    rhs_q = spread(rhs_parts)
    (pivot_parts,) = gather([jnp.sum(picks, axis=0)], "panel", 1)
    pivot_rows = pivot_parts.reshape(-1, points.shape[0])
    pivot_sq = jnp.sum(pivot_rows * pivot_rows, axis=1)

    panel_q = kern(pivot_rows, pivot_sq, visit, 1, visit_sq)
    panel_own = kern(pivot_rows, pivot_sq, scaled, 0, local_sq)
    inner_kernel = kern(pivot_rows, pivot_sq, pivot_rows, 1, pivot_sq)
    sums = [dot(panel_q, panel_q, 1, 1), dot(rhs_q, panel_q, 1, 1)]
    if 4 * visit.shape[0] * row_count <= LOOP_BYTES // 3:
        gram, proj, high, low = sum_over(
            sums, "panel", 2, (visit, scaled, local_sq[None, :]), quarter
        )
        inverse = inverse_of(noise * inner_kernel + gram)
        return tuple(
            loop_of(
                proj, inverse, rhs_q, right_sides, panel_q, panel_own, high, low,
                noise_level.reshape(1, 1),
            )
        )
    tile = kern(visit, visit_sq, scaled, 0, local_sq)
    gram, proj = sum_over(sums, "panel", 2)
    inverse = inverse_of(noise * inner_kernel + gram)

    def coefficients_of(projected):
        return dot(projected, inverse, 1, 0, FULL)

    def precondition(resid, coefficients, panel_rows):
        return (resid - dot(coefficients, panel_rows, 1, 0)) / noise

    coef = coefficients_of(proj)
    dir_q = precondition(rhs_q, coef, panel_q)
    dir_own = precondition(right_sides, coef, panel_own)
    (image_own,) = sum_over([dot(dir_q, tile, 1, 0)], "panel", 3)
    image_own = image_own + noise * dir_own
    (image_parts,) = gather([own_quarter(image_own)], "blk", 4)
    image_q = spread(image_parts)
    lanes = lax.broadcasted_iota(jnp.int32, (1, 128), 1)

    def pack(columns):
        packed = jnp.zeros((vec, 128), jnp.float32)
        for index, column in enumerate(columns):
            packed = jnp.where(lanes == index, column[:, None], packed)
        return packed

    image_proj, dots = sum_over(
        [
            dot(image_q, panel_q, 1, 1),
            pack([jnp.sum(rhs_q * dir_q, axis=1), jnp.sum(dir_q * image_q, axis=1)]),
        ],
        "panel",
        5,
    )
    norm, curvature = dots[:, 0], dots[:, 1]
    step = (norm / curvature)[:, None]
    coef = coefficients_of(proj - step * image_proj)
    resid_own = right_sides - step * image_own
    pre_q = precondition(rhs_q - step * image_q, coef, panel_q)
    pre_own = precondition(resid_own, coef, panel_own)
    (pre_image,) = sum_over([dot(pre_q, tile, 1, 0)], "panel", 6)
    pre_image = pre_image + noise * pre_own
    (dot_parts,) = gather(
        [
            pack(
                [
                    jnp.sum(resid_own * pre_own, axis=1),
                    jnp.sum(pre_own * pre_image, axis=1),
                    jnp.sum(pre_own * image_own + dir_own * pre_image, axis=1),
                ]
            )
        ],
        "blk",
        7,
    )
    dots = jnp.sum(dot_parts, axis=0)
    new_norm = dots[:, 0]
    ratio = new_norm / norm
    curvature = dots[:, 1] + ratio * (dots[:, 2] + ratio * curvature)
    last = (new_norm / curvature)[:, None]
    ratio = ratio[:, None]
    solution = step * dir_own + last * (pre_own + ratio * dir_own)
    residual = resid_own - last * (pre_image + ratio * image_own)
    return (solution, residual)


def solution(mesh):
    return jax.shard_map(
        per_device,
        mesh=mesh,
        in_specs=(P(None, "blk"), P(), P(), P(None, "blk"), P("panel")),
        out_specs=(P(None, "blk"), P(None, "blk")),
        check_vma=False,
    )
```

```python
import functools

import jax
import jax.numpy as jnp
from jax import lax
from jax.experimental import pallas as pl
from jax.experimental.pallas import tpu as pltpu
from jax.sharding import PartitionSpec as P

FULL = lax.Precision.HIGHEST
VMEM = pl.BlockSpec(memory_space=pltpu.VMEM)
MESH = pl.DeviceIdType.MESH
VMEM_BYTES = 16 * 1024 * 1024
LOOP_BYTES = 28 * 1024 * 1024


def dot(left, right, left_dim, right_dim, precision=lax.Precision.HIGH):
    return lax.dot_general(
        left,
        right,
        (((left_dim,), (right_dim,)), ((), ())),
        precision=precision,
        preferred_element_type=jnp.float32,
    )


def gather_kernel(axis, size, count, *refs):
    ins, outs = refs[:count], refs[count : 2 * count]
    send_sem, recv_sem = refs[2 * count :]
    me = lax.axis_index(axis)
    barrier = pltpu.get_barrier_semaphore()
    for hop in range(1, size):
        pl.semaphore_signal(
            barrier, inc=1, device_id={axis: lax.rem(me + hop, size)}, device_id_type=MESH
        )
    pl.semaphore_wait(barrier, size - 1)

    def copy_of(item, hop, slot):
        return pltpu.make_async_remote_copy(
            src_ref=ins[item],
            dst_ref=outs[item].at[slot],
            send_sem=send_sem.at[item, hop],
            recv_sem=recv_sem.at[item, hop],
            device_id={axis: lax.rem(me + hop, size)},
            device_id_type=MESH,
        )

    for hop in range(size - 1, 0, -1):
        for item in range(count):
            copy_of(item, hop, me).start()
    for item in range(count):
        outs[item][me] = ins[item][...]
    for hop in range(1, size):
        for item in range(count):
            copy_of(item, hop, lax.rem(me + size - hop, size)).wait_recv()
    for hop in range(1, size):
        for item in range(count):
            copy_of(item, hop, me).wait_send()


def gather(arrays, axis, collective_id):
    size = lax.axis_size(axis)
    count = len(arrays)
    return pl.pallas_call(
        functools.partial(gather_kernel, axis, size, count),
        out_shape=[jax.ShapeDtypeStruct((size,) + a.shape, a.dtype) for a in arrays],
        in_specs=[VMEM] * count,
        out_specs=[VMEM] * count,
        scratch_shapes=[
            pltpu.SemaphoreType.DMA((count, size)),
            pltpu.SemaphoreType.DMA((count, size)),
        ],
        compiler_params=pltpu.CompilerParams(
            collective_id=collective_id, has_side_effects=True, vmem_limit_bytes=VMEM_BYTES
        ),
    )(*arrays)


def forward_kernel(axis, size, count, *refs):
    ins, outs = refs[:count], refs[count : 2 * count]
    up_send, up_recv, down_send, down_recv, pair_send, pair_recv = refs[2 * count :]
    half = size // 2
    me = lax.axis_index(axis)
    place = me // 2
    partner = me + 1 - 2 * lax.rem(me, 2)
    has_above, has_below = place < half - 1, place > 0
    barrier = pltpu.get_barrier_semaphore()

    def greet(device):
        pl.semaphore_signal(barrier, inc=1, device_id={axis: device}, device_id_type=MESH)

    greet(partner)
    pl.when(has_above)(lambda: greet(me + 2))
    pl.when(has_below)(lambda: greet(me - 2))
    pl.semaphore_wait(barrier, 1 + has_above.astype(jnp.int32) + has_below.astype(jnp.int32))

    def copies(own, slot, sends, recvs, index, device):
        return [
            pltpu.make_async_remote_copy(
                src_ref=ins[item] if own else outs[item].at[slot],
                dst_ref=outs[item].at[slot],
                send_sem=sends.at[item, index],
                recv_sem=recvs.at[item, index],
                device_id={axis: device},
                device_id_type=MESH,
            )
            for item in range(count)
        ]

    def up(distance):
        slot = me - 2 * (distance - 1)
        return copies(distance == 1, slot, up_send, up_recv, distance, me + 2)

    def down(distance):
        slot = me + 2 * (distance - 1)
        return copies(distance == 1, slot, down_send, down_recv, distance, me - 2)

    def pair(shift):
        index = abs(shift) if shift <= 0 else half - 1 + shift
        return copies(shift == 0, me + 2 * shift, pair_send, pair_recv, index, partner)

    def start(group):
        for copy in group:
            copy.start()

    def arrived(group_of, slot, sends, recvs, index):
        for copy in copies(False, slot, sends, recvs, index, group_of):
            copy.wait_recv()

    pl.when(has_above)(lambda: start(up(1)))
    pl.when(has_below)(lambda: start(down(1)))
    start(pair(0))
    for item in range(count):
        outs[item][me] = ins[item][...]
    for distance in range(1, half):

        @pl.when(place - distance >= 0)
        def _():
            arrived(partner, me - 2 * distance, up_send, up_recv, distance)
            if distance < half - 1:
                pl.when(has_above)(lambda: start(up(distance + 1)))
            start(pair(-distance))

        @pl.when(place + distance <= half - 1)
        def _():
            arrived(partner, me + 2 * distance, down_send, down_recv, distance)
            if distance < half - 1:
                pl.when(has_below)(lambda: start(down(distance + 1)))
            start(pair(distance))

    def sent(group):
        for copy in group:
            copy.wait_send()

    def settle(shift):
        index = abs(shift) if shift <= 0 else half - 1 + shift
        arrived(partner, partner + 2 * shift, pair_send, pair_recv, index)
        sent(pair(shift))

    settle(0)
    pl.when(has_above)(lambda: sent(up(1)))
    pl.when(has_below)(lambda: sent(down(1)))
    for distance in range(1, half):

        @pl.when(place - distance >= 0)
        def _():
            settle(-distance)
            if distance < half - 1:
                pl.when(has_above)(lambda: sent(up(distance + 1)))

        @pl.when(place + distance <= half - 1)
        def _():
            settle(distance)
            if distance < half - 1:
                pl.when(has_below)(lambda: sent(down(distance + 1)))


def forward_gather(arrays, axis, collective_id):
    size = lax.axis_size(axis)
    count = len(arrays)
    return pl.pallas_call(
        functools.partial(forward_kernel, axis, size, count),
        out_shape=[jax.ShapeDtypeStruct((size,) + a.shape, a.dtype) for a in arrays],
        in_specs=[VMEM] * count,
        out_specs=[VMEM] * count,
        scratch_shapes=[pltpu.SemaphoreType.DMA((count, size))] * 6,
        compiler_params=pltpu.CompilerParams(
            collective_id=collective_id, has_side_effects=True, vmem_limit_bytes=VMEM_BYTES
        ),
    )(*arrays)


def tile_rows(refs, first, last, chunk):
    visit_ref, scaled_ref, sq_ref, high_ref, low_ref = refs

    def one(index, carry):
        rows = pl.ds(pl.multiple_of(index * chunk, 16), chunk)
        left = visit_ref[rows, :]
        cross = dot(left, scaled_ref[...], 1, 0, FULL)
        left_sq = jnp.sum(left * left, axis=1, keepdims=True)
        values = jnp.exp(-0.5 * (left_sq + sq_ref[...] - 2.0 * cross))
        high = values.astype(jnp.bfloat16)
        high_ref[rows, :] = high
        low_ref[rows, :] = (values - high.astype(jnp.float32)).astype(jnp.bfloat16)
        return carry

    lax.fori_loop(first, last, one, 0)


def sum_kernel(axis, steps, count, chunk, *refs):
    extra = 3 if chunk else 0
    ins, outs = refs[:count], refs[count + extra : 2 * count + extra]
    made = 2 * count + extra
    tile_refs = refs[count : count + extra] + refs[made : made + (2 if chunk else 0)]
    refs = refs[made + (2 if chunk else 0) :]
    landed = refs[:count]
    send_sem, recv_sem = refs[count:]
    me = lax.axis_index(axis)
    partners = [me + s * (1 - 2 * lax.rem(me // s, 2)) for s in steps]
    barrier = pltpu.get_barrier_semaphore()
    for partner in partners:
        pl.semaphore_signal(barrier, inc=1, device_id={axis: partner}, device_id_type=MESH)
    pl.semaphore_wait(barrier, len(steps))
    held = list(ins)
    for step, partner in enumerate(partners):
        copies = []
        for item in range(count):
            copy = pltpu.make_async_remote_copy(
                src_ref=held[item],
                dst_ref=landed[item].at[step],
                send_sem=send_sem.at[item, step],
                recv_sem=recv_sem.at[item, step],
                device_id={axis: partner},
                device_id_type=MESH,
            )
            copy.start()
            copies.append(copy)
        if chunk:
            pieces = tile_refs[0].shape[0] // chunk
            cut = [pieces * (step + i) // len(steps) for i in (0, 1)]
            tile_rows(tile_refs, cut[0], cut[1], chunk)
        for item in range(count):
            copies[item].wait()
            outs[item][...] = held[item][...] + landed[item][step]
            held[item] = outs[item]


def sum_over(arrays, axis, collective_id, tile_of=(), chunk=0):
    size = lax.axis_size(axis)
    steps = []
    while (1 << len(steps)) < size:
        steps.append(1 << len(steps))
    count = len(arrays)
    halves = []
    if chunk:
        shape = (tile_of[0].shape[0], tile_of[1].shape[1])
        halves = [jax.ShapeDtypeStruct(shape, jnp.bfloat16)] * 2
    return pl.pallas_call(
        functools.partial(sum_kernel, axis, steps, count, chunk),
        out_shape=[jax.ShapeDtypeStruct(a.shape, a.dtype) for a in arrays] + halves,
        in_specs=[VMEM] * (count + len(tile_of)),
        out_specs=[VMEM] * (count + len(halves)),
        scratch_shapes=[pltpu.VMEM((len(steps),) + a.shape, a.dtype) for a in arrays]
        + [
            pltpu.SemaphoreType.DMA((count, len(steps))),
            pltpu.SemaphoreType.DMA((count, len(steps))),
        ],
        compiler_params=pltpu.CompilerParams(
            collective_id=collective_id, has_side_effects=True, vmem_limit_bytes=VMEM_BYTES
        ),
    )(*arrays, *tile_of)


def inverse_kernel(side, part, width, a_ref, out_ref):
    sub = lax.broadcasted_iota(jnp.int32, (part, part), 0)
    lane = lax.broadcasted_iota(jnp.int32, (part, part), 1)
    head = lax.broadcasted_iota(jnp.int32, (1, part), 1)
    out_ref[...] = a_ref[...]

    def block_step(_, carry):
        block = out_ref[:part, :part]
        for first in range(0, part, width):
            columns = [
                jnp.broadcast_to(block[:, k : k + 1], (part, part))
                for k in range(first, first + width)
            ]
            for index in range(width):
                k = first + index
                here = sub == k
                column = columns[index]
                scale = 1.0 / column[k : k + 1, :]
                row = jnp.where(head == k, 1.0, block[k : k + 1, :]) * scale
                factor = jnp.where(here, -1.0, column)
                block = jnp.where(here | (lane == k), 0.0, block) - factor * row
                for later in range(index + 1, width):
                    entry = columns[later][k : k + 1, :] * scale
                    columns[later] = jnp.where(here, 0.0, columns[later]) - factor * entry
        left = out_ref[part:, :part]
        right = dot(block, out_ref[:part, part:], 1, 0, FULL)
        rest = out_ref[part:, part:] - dot(left, right, 1, 0, FULL)
        side_part = -dot(left, block, 1, 0, FULL)
        out_ref[...] = jnp.concatenate(
            [
                jnp.concatenate([rest, side_part], axis=1),
                jnp.concatenate([right, block], axis=1),
            ],
            axis=0,
        )
        return carry

    lax.fori_loop(0, side // part, block_step, 0)


def inverse_of(matrix):
    side = matrix.shape[0]
    return pl.pallas_call(
        functools.partial(inverse_kernel, side, 64, 8),
        out_shape=jax.ShapeDtypeStruct(matrix.shape, matrix.dtype),
        in_specs=[VMEM],
        out_specs=VMEM,
        compiler_params=pltpu.CompilerParams(vmem_limit_bytes=VMEM_BYTES),
    )(matrix)


def kern(left, left_sq, right, right_dim, right_sq):
    cross = dot(left, right, 1, right_dim, FULL)
    return jnp.exp(-0.5 * (left_sq[:, None] + right_sq[None, :] - 2.0 * cross))


def loop_kernel(size, panel_size, vec, quarter, *refs):
    proj_ref, inverse_ref, rhs_visit, rhs_own, panel_visit, panel_own = refs[:6]
    high_ref, low_ref, noise_ref, solution_ref, residual_ref = refs[6:11]
    first_sum, second_sum, image_parts, dot_sum, last_sum = refs[11:16]
    send_sem, recv_sem = refs[16:]
    row, column = lax.axis_index("blk"), lax.axis_index("panel")
    rank = proj_ref.shape[1]
    barrier = pltpu.get_barrier_semaphore()
    for hop in range(1, size):
        pl.semaphore_signal(
            barrier, inc=1, device_id={"blk": lax.rem(row + hop, size)}, device_id_type=MESH
        )
    for hop in range(1, panel_size):
        pl.semaphore_signal(
            barrier,
            inc=1,
            device_id={"panel": lax.rem(column + hop, panel_size)},
            device_id_type=MESH,
        )
    noise = noise_ref[...]

    def exchange(axis, buffer, phase, beside=None):
        me, count = (row, size) if axis == "blk" else (column, panel_size)

        def copy_of(hop, slot):
            return pltpu.make_async_remote_copy(
                src_ref=buffer.at[slot],
                dst_ref=buffer.at[slot],
                send_sem=send_sem.at[phase, hop],
                recv_sem=recv_sem.at[phase, hop],
                device_id={axis: lax.rem(me + hop, count)},
                device_id_type=MESH,
            )

        for hop in range(count - 1, 0, -1):
            copy_of(hop, me).start()
        result = beside() if beside else None
        for hop in range(1, count):
            copy_of(hop, lax.rem(me + count - hop, count)).wait_recv()
        for hop in range(1, count):
            copy_of(hop, me).wait_send()
        return result

    def total_of(buffer, count):
        total = buffer[0]
        for index in range(1, count):
            total = total + buffer[index]
        return total

    def precondition(resid, coefficients, panel_rows):
        return (resid - dot(coefficients, panel_rows, 1, 0, FULL)) / noise

    def tile_product(vectors):
        high = vectors.astype(jnp.bfloat16)
        low = (vectors - high.astype(jnp.float32)).astype(jnp.bfloat16)
        product = jnp.zeros(rhs_own.shape, jnp.float32)
        for left, right in ((high, high_ref), (low, high_ref), (high, low_ref)):
            product = product + lax.dot_general(
                left,
                right[...],
                (((1,), (0,)), ((), ())),
                preferred_element_type=jnp.float32,
            )
        return product

    def row_sum(left, right):
        return jnp.sum(left * right, axis=1, keepdims=True)

    lanes = lax.broadcasted_iota(jnp.int32, (vec, 128), 1)

    def pack(columns):
        packed = jnp.zeros((vec, 128), jnp.float32)
        for index, value in enumerate(columns):
            packed = jnp.where(lanes == index, value, packed)
        return packed

    coef = dot(proj_ref[...], inverse_ref[...], 1, 0, FULL)
    dir_visit = precondition(rhs_visit[...], coef, panel_visit[...])
    first_sum[column] = tile_product(dir_visit)
    pl.semaphore_wait(barrier, size + panel_size - 2)
    dir_own = exchange(
        "panel", first_sum, 0, lambda: precondition(rhs_own[...], coef, panel_own[...])
    )
    image_own = total_of(first_sum, panel_size) + noise * dir_own
    for index in range(panel_size):

        @pl.when(column == index)
        def _():
            image_parts[row] = image_own[:, index * quarter : (index + 1) * quarter]

    exchange("blk", image_parts, 1)
    image_visit = jnp.concatenate([image_parts[index] for index in range(size)], axis=1)
    image_proj = dot(image_visit, panel_visit[...], 1, 1, FULL)
    norm = row_sum(rhs_visit[...], dir_visit)
    curvature = row_sum(dir_visit, image_visit)
    dot_sum[column, :, :rank] = image_proj
    dot_sum[column, :, rank:] = pack([norm, curvature])
    exchange("panel", dot_sum, 2)
    totals = total_of(dot_sum, panel_size)
    image_proj = totals[:, :rank]
    norm, curvature = totals[:, rank : rank + 1], totals[:, rank + 1 : rank + 2]
    step = norm / curvature
    coef = dot(proj_ref[...] - step * image_proj, inverse_ref[...], 1, 0, FULL)
    pre_visit = precondition(rhs_visit[...] - step * image_visit, coef, panel_visit[...])
    second_sum[column] = tile_product(pre_visit)
    resid_own = rhs_own[...] - step * image_own
    pre_own = exchange(
        "panel", second_sum, 3, lambda: precondition(resid_own, coef, panel_own[...])
    )
    pre_image = total_of(second_sum, panel_size) + noise * pre_own
    last_sum[row] = pack(
        [
            row_sum(resid_own, pre_own),
            row_sum(pre_own, pre_image),
            row_sum(pre_own, image_own) + row_sum(dir_own, pre_image),
        ]
    )
    exchange("blk", last_sum, 4)
    totals = total_of(last_sum, size)
    new_norm = totals[:, 0:1]
    ratio = new_norm / norm
    curvature = totals[:, 1:2] + ratio * (totals[:, 2:3] + ratio * curvature)
    last = new_norm / curvature
    solution_ref[...] = step * dir_own + last * (pre_own + ratio * dir_own)
    residual_ref[...] = resid_own - last * (pre_image + ratio * image_own)


def loop_of(proj, inverse, rhs_visit, rhs_own, panel_visit, panel_own, high, low, noise):
    size, panel_size = lax.axis_size("blk"), lax.axis_size("panel")
    vec, rank = proj.shape
    quarter = rhs_visit.shape[1] // size
    most = max(size, panel_size)
    own = jax.ShapeDtypeStruct(rhs_own.shape, jnp.float32)
    return pl.pallas_call(
        functools.partial(loop_kernel, size, panel_size, vec, quarter),
        out_shape=[own, own],
        in_specs=[VMEM] * 9,
        out_specs=[VMEM] * 2,
        scratch_shapes=[
            pltpu.VMEM((panel_size,) + rhs_own.shape, jnp.float32),
            pltpu.VMEM((panel_size,) + rhs_own.shape, jnp.float32),
            pltpu.VMEM((size, vec, quarter), jnp.float32),
            pltpu.VMEM((panel_size, vec, rank + 128), jnp.float32),
            pltpu.VMEM((size, vec, 128), jnp.float32),
            pltpu.SemaphoreType.DMA((5, most)),
            pltpu.SemaphoreType.DMA((5, most)),
        ],
        compiler_params=pltpu.CompilerParams(
            collective_id=8, has_side_effects=True, vmem_limit_bytes=LOOP_BYTES
        ),
    )(proj, inverse, rhs_visit, rhs_own, panel_visit, panel_own, high, low, noise)


def per_device(points, lengthscale, noise_level, right_sides, pivots):
    row_count = points.shape[1]
    vec = right_sides.shape[0]
    panel_size = lax.axis_size("panel")
    quarter = row_count // panel_size
    panel_start = lax.axis_index("panel") * quarter
    noise = noise_level[0]
    scaled = points / lengthscale[:, None]
    local_sq = jnp.sum(scaled * scaled, axis=0)
    row_ids = lax.axis_index("blk") * row_count + lax.iota(jnp.int32, row_count)
    onehot = (pivots[:, None] == row_ids[None, :]).astype(jnp.float32)
    picked = dot(onehot, scaled, 1, 1, FULL)

    def own_quarter(vectors):
        return lax.dynamic_slice_in_dim(vectors, panel_start, quarter, 1)

    def spread(stacked):
        return stacked.transpose(1, 0, 2).reshape(vec, -1)

    quarter_points, picks, rhs_parts = forward_gather(
        [own_quarter(scaled).T, picked, own_quarter(right_sides)], "blk", 0
    )
    visit = quarter_points.reshape(-1, points.shape[0])
    visit_sq = jnp.sum(visit * visit, axis=1)
    rhs_q = spread(rhs_parts)
    (pivot_parts,) = gather([jnp.sum(picks, axis=0)], "panel", 1)
    pivot_rows = pivot_parts.reshape(-1, points.shape[0])
    pivot_sq = jnp.sum(pivot_rows * pivot_rows, axis=1)

    panel_q = kern(pivot_rows, pivot_sq, visit, 1, visit_sq)
    panel_own = kern(pivot_rows, pivot_sq, scaled, 0, local_sq)
    inner_kernel = kern(pivot_rows, pivot_sq, pivot_rows, 1, pivot_sq)
    sums = [dot(panel_q, panel_q, 1, 1), dot(rhs_q, panel_q, 1, 1)]
    if 4 * visit.shape[0] * row_count <= LOOP_BYTES // 3:
        gram, proj, high, low = sum_over(
            sums, "panel", 2, (visit, scaled, local_sq[None, :]), quarter
        )
        inverse = inverse_of(noise * inner_kernel + gram)
        return tuple(
            loop_of(
                proj, inverse, rhs_q, right_sides, panel_q, panel_own, high, low,
                noise_level.reshape(1, 1),
            )
        )
    tile = kern(visit, visit_sq, scaled, 0, local_sq)
    gram, proj = sum_over(sums, "panel", 2)
    inverse = inverse_of(noise * inner_kernel + gram)

    def coefficients_of(projected):
        return dot(projected, inverse, 1, 0, FULL)

    def precondition(resid, coefficients, panel_rows):
        return (resid - dot(coefficients, panel_rows, 1, 0)) / noise

    coef = coefficients_of(proj)
    dir_q = precondition(rhs_q, coef, panel_q)
    dir_own = precondition(right_sides, coef, panel_own)
    (image_own,) = sum_over([dot(dir_q, tile, 1, 0)], "panel", 3)
    image_own = image_own + noise * dir_own
    (image_parts,) = gather([own_quarter(image_own)], "blk", 4)
    image_q = spread(image_parts)
    lanes = lax.broadcasted_iota(jnp.int32, (1, 128), 1)

    def pack(columns):
        packed = jnp.zeros((vec, 128), jnp.float32)
        for index, column in enumerate(columns):
            packed = jnp.where(lanes == index, column[:, None], packed)
        return packed

    image_proj, dots = sum_over(
        [
            dot(image_q, panel_q, 1, 1),
            pack([jnp.sum(rhs_q * dir_q, axis=1), jnp.sum(dir_q * image_q, axis=1)]),
        ],
        "panel",
        5,
    )
    norm, curvature = dots[:, 0], dots[:, 1]
    step = (norm / curvature)[:, None]
    coef = coefficients_of(proj - step * image_proj)
    resid_own = right_sides - step * image_own
    pre_q = precondition(rhs_q - step * image_q, coef, panel_q)
    pre_own = precondition(resid_own, coef, panel_own)
    (pre_image,) = sum_over([dot(pre_q, tile, 1, 0)], "panel", 6)
    pre_image = pre_image + noise * pre_own
    (dot_parts,) = gather(
        [
            pack(
                [
                    jnp.sum(resid_own * pre_own, axis=1),
                    jnp.sum(pre_own * pre_image, axis=1),
                    jnp.sum(pre_own * image_own + dir_own * pre_image, axis=1),
                ]
            )
        ],
        "blk",
        7,
    )
    dots = jnp.sum(dot_parts, axis=0)
    new_norm = dots[:, 0]
    ratio = new_norm / norm
    curvature = dots[:, 1] + ratio * (dots[:, 2] + ratio * curvature)
    last = (new_norm / curvature)[:, None]
    ratio = ratio[:, None]
    solution = step * dir_own + last * (pre_own + ratio * dir_own)
    residual = resid_own - last * (pre_image + ratio * image_own)
    return (solution, residual)


def solution(mesh):
    return jax.shard_map(
        per_device,
        mesh=mesh,
        in_specs=(P(None, "blk"), P(), P(), P(None, "blk"), P("panel")),
        out_specs=(P(None, "blk"), P(None, "blk")),
        check_vma=False,
    )
```
